512 devices in a mesh: graph: 16 (over z), row: 32 (over x, y, core).
Axes of the slice: x: 4, y: 4, z: 16, core: 2. Of those that a mesh axis runs over, the one named last changes fastest.
Arguments:
- pair: bfloat16 [6144, 384, 128], P(('graph', 'row')), parts along dimension 0, may hold values from -6 to 6
- edge_type: int32 [6144, 384], P(('graph', 'row')), parts along dimension 0, may hold values from 0 to 7
- node_mask: int32 [6144], P('graph'), parts along dimension 0, may hold values 0 or 1
- type_table: bfloat16 [8, 128], replicated, may hold values from -6 to 6
- in_gain: float32 [2, 128], replicated, may hold values from 0.1 to 1.9
- proj_weight: bfloat16 [2, 128, 512], replicated, may hold values from -0.5 to 0.5
- gate_weight: bfloat16 [2, 128, 128], replicated, may hold values from -0.5 to 0.5
- out_gain: float32 [2, 128], replicated, may hold values from 0.1 to 1.9
- out_weight: bfloat16 [2, 128, 128], replicated, may hold values from -0.5 to 0.5
Outputs:
- result: bfloat16 [6144, 384, 128], P(('graph', 'row')), parts along dimension 0
The draws below stay inside these ranges and needn't reach their ends.
There are 16 independent parts, one for each index of `graph`. The reference program is written for one: setup_inputs(seed, part) draws one part's arguments, and reference() takes and returns one part's arrays. A program takes and returns all parts, laid end to end along the dimension named above; an argument that names none is the same for every part. Nothing has to cross between parts.
All inputs are finite; a program needn't handle non-finite values.
Results may differ from the reference program's by a relative error of at most 0.012.
Values may be sent and summed in bfloat16 or wider, within the bound.
No kernel may reach another device: no remote copies, remote signals or barrier semaphores. Data moves between devices by JAX's collectives and lax.ppermute only.
A program may use at most 64 MiB of HBM per device.

```python
import jax
import jax.numpy as jnp
from jax import lax

N = 384
C = 128
HID = 128
NTYPES = 8


def set_ends(drawn, key, smallest, largest):
    extent = drawn.shape
    index_at = [jax.random.randint(jax.random.fold_in(key, axis), (), 0, extent[axis]) for axis in range(len(extent))]
    drawn = drawn.at[tuple(index_at)].set(smallest)
    longest = extent.index(max(extent))
    index_at[longest] = (index_at[longest] + 1) % extent[longest]
    return drawn.at[tuple(index_at)].set(largest)


def levels(key, shape, split, least, largest):
    factor_of, own = 1.0, jax.random.fold_in(key, 6)
    for axis_at, blocks in split:
        heights = jnp.exp(jax.random.uniform(jax.random.fold_in(own, axis_at), (blocks,), jnp.float32, least / len(split), largest / len(split)))
        factor_of = factor_of * jnp.repeat(heights, shape[axis_at] // blocks).reshape([-1 if axis == axis_at else 1 for axis in range(len(shape))])
    return factor_of


def normal_values(stream_key, shape, deviation, limit, cuts=(), held_as=jnp.bfloat16):
    factor_of = levels(stream_key, shape, cuts, -0.22, 0.18) if cuts else 1.0
    result = jax.random.normal(stream_key, shape, jnp.float32) * deviation * factor_of
    return jnp.minimum(jnp.maximum(result, -limit), limit).astype(held_as)


def setup_inputs(seed: int = 0, part: int = 0) -> dict:
    key_of = jax.random.split(jax.random.key(seed), 10)
    own_keys = jax.random.split(jax.random.fold_in(key_of[9], part), 10)
    return {
        "pair": normal_values(own_keys[0], (N, N, C), 1.0, 6.0, ((0, 32),)),
        "edge_type": set_ends(jax.random.randint(own_keys[1], (N, N), 0, NTYPES), jax.random.fold_in(own_keys[1], 1), 0, NTYPES - 1).astype(jnp.int32),
        "node_mask": set_ends((jax.random.randint(own_keys[2], (N,), 0, 8) < 7).astype(jnp.int32), jax.random.fold_in(own_keys[2], 1), 0, 1),
        "type_table": normal_values(key_of[3], (NTYPES, C), 1.0, 6.0),
        "in_gain": jnp.clip(1.0 + 0.18 * jax.random.normal(key_of[4], (2, C), jnp.float32), 0.1, 1.9),
        "proj_weight": normal_values(key_of[5], (2, C, 4 * HID), C ** -0.5, 0.5),
        "gate_weight": normal_values(key_of[6], (2, C, C), C ** -0.5, 0.5),
        "out_gain": jnp.clip(1.0 + 0.18 * jax.random.normal(key_of[7], (2, HID), jnp.float32), 0.1, 1.9),
        "out_weight": normal_values(key_of[8], (2, HID, C), HID ** -0.5, 0.5),
    }


def layer_norm(value, gain):
    mean = lax.optimization_barrier(jnp.mean(value, axis=-1, keepdims=True))
    centered = value - mean
    var = lax.optimization_barrier(jnp.mean(centered * centered, axis=-1, keepdims=True))
    return centered * lax.rsqrt(var + 1e-05) * gain

def reference(pair, edge_type, node_mask, type_table, in_gain, proj_weight, gate_weight, out_gain, out_weight):
    table_rows = type_table.astype(jnp.float32)[edge_type]
    z = (pair.astype(jnp.float32) + table_rows).astype(jnp.bfloat16)
    maskf = node_mask.astype(jnp.float32)
    pair_mask = maskf[:, None] * maskf[None, :]
    for layer in range(2):
        zf = z.astype(jnp.float32)
        normed = layer_norm(zf, in_gain[layer]).astype(jnp.bfloat16)
        flat = normed.reshape(N * N, C)
        proj = jnp.dot(flat, proj_weight[layer], preferred_element_type=jnp.float32).reshape(N, N, 4 * HID)
        left = (jax.nn.sigmoid(proj[..., :HID]) * proj[..., HID:2 * HID] * pair_mask[..., None]).astype(jnp.bfloat16)
        right = (jax.nn.sigmoid(proj[..., 2 * HID:3 * HID]) * proj[..., 3 * HID:] * pair_mask[..., None]).astype(jnp.bfloat16)
        leftf = left.astype(jnp.float32)
        rightf = right.astype(jnp.float32)
        if layer == 0:
            tri = jnp.einsum('ikc,jkc->ijc', leftf, rightf, precision=lax.Precision.HIGHEST)
        else:
            tri = jnp.einsum('kic,kjc->ijc', leftf, rightf, precision=lax.Precision.HIGHEST)
        tri = tri.astype(jnp.bfloat16)
        tri_norm = layer_norm(tri.astype(jnp.float32), out_gain[layer]).astype(jnp.bfloat16)
        update = jnp.dot(tri_norm.reshape(N * N, HID), out_weight[layer], preferred_element_type=jnp.float32)
        gate = jax.nn.sigmoid(jnp.dot(flat, gate_weight[layer], preferred_element_type=jnp.float32))
        z = (zf + (gate * update).reshape(N, N, C)).astype(jnp.bfloat16)
    return z
```

```python
import jax
import jax.numpy as jnp
from jax import lax
from jax.experimental import pallas as pl
from jax.experimental.pallas import tpu as pltpu
from jax.sharding import PartitionSpec as P

F32 = jnp.float32
BF16 = jnp.bfloat16
STEP = 4
NT = (((1,), (1,)), ((), ()))
TN = (((0,), (0,)), ((), ()))


def dot(lhs, rhs):
    return jnp.dot(lhs, rhs, preferred_element_type=F32)


def iotas(rows, cols):
    return lax.broadcasted_iota(jnp.int32, (rows, cols), 0), lax.broadcasted_iota(
        jnp.int32, (rows, cols), 1
    )


def eye(n):
    row, col = iotas(n, n)
    return (row == col).astype(BF16)


def swap_matrix(n, outer, inner):
    row, col = iotas(n, n)
    return (col == (row % inner) * outer + row // inner).astype(BF16)


def norm_channels(value, gain):
    chans = value.shape[0]
    mean = jnp.sum(value, axis=0, keepdims=True) * (1.0 / chans)
    centered = value - mean
    var = jnp.sum(centered * centered, axis=0, keepdims=True) * (1.0 / chans)
    return centered * lax.rsqrt(var + 1e-05) * gain


def prepare_in(gain_ref, proj_ref, gain_s, proj_s, layer, groups):
    chans = gain_ref.shape[1]
    wide = proj_ref.shape[1]
    hidden = wide // 4
    per = hidden // groups
    gain = jnp.broadcast_to(gain_ref[layer : layer + 1, :], (chans, chans)).T
    gain_s[...] = jnp.concatenate([gain] * (gain_s.shape[1] // chans), axis=1)
    row, col = iotas(wide, wide)
    kind = row // (2 * hidden)
    group = (row // (2 * per)) % groups
    side = (row // per) % 2
    source = side * (2 * hidden) + kind * hidden + group * per + row % per
    pick = jnp.where(col == source, jnp.where(kind == 0, 0.5, 1.0), 0.0).astype(BF16)
    proj_s[...] = lax.dot_general(pick, proj_ref[...], NT, preferred_element_type=F32).astype(BF16)


def emit_factors(rows_z, first, start_ref, mask_smem, mask_ref, gain_s, proj_s, z_ref, normed_ref, ab_ref, groups):
    nodes = mask_ref.shape[1]
    lane_mask = mask_ref[...].astype(F32) * 0.5
    done = []
    for r, z in enumerate(rows_z):
        z_ref[r] = z
        normed = norm_channels(z.astype(F32), gain_s[...]).astype(BF16)
        normed_ref[r] = normed
        proj = dot(proj_s[...], normed)
        half = proj.shape[0] // 2
        row_mask = mask_smem[start_ref[0] + first + r].astype(F32)
        ab = (jnp.tanh(proj[:half]) + 1.0) * proj[half:] * (lane_mask * row_mask)
        done.append(ab.reshape(groups, half // groups, nodes))
        if r % 2:
            both = jnp.concatenate(done, axis=1).astype(BF16)
            height = both.shape[1]
            ab_ref[:, (r // 2) * height : (r // 2 + 1) * height, :] = both
            done = []


def first_kernel(
    start_ref, mask_smem, pair_ref, edge_ref, mask_ref, table_ref, gain_ref, proj_ref,
    ab_ref, z_ref, normed_ref, gain_s, proj_s,
):
    step = pl.program_id(0)
    groups = ab_ref.shape[0]

    @pl.when(step == 0)
    def _():
        prepare_in(gain_ref, proj_ref.at[0], gain_s, proj_s, 0, groups)

    kinds, chans = table_ref.shape
    nodes = mask_ref.shape[1]
    ident = eye(chans)
    table = table_ref[...]
    rows_z = []
    for r in range(STEP):
        edges = edge_ref[pl.ds(step * STEP + r, 1), :]
        onehot = (lax.broadcasted_iota(jnp.int32, (kinds, nodes), 0) == edges).astype(BF16)
        added = lax.dot_general(table, onehot, TN, preferred_element_type=F32)
        pair = lax.dot_general(ident, pair_ref[r], NT, preferred_element_type=F32)
        rows_z.append((pair + added).astype(BF16))
    emit_factors(rows_z, step * STEP, start_ref, mask_smem, mask_ref, gain_s, proj_s, z_ref, normed_ref, ab_ref, groups)


def prepare_out(gain_ref, weight_ref, gain_s, weight_s, layer):
    chans = gain_ref.shape[1]
    gain = jnp.broadcast_to(gain_ref[layer : layer + 1, :], (chans, chans)).T
    gain_s[...] = jnp.concatenate([gain] * (gain_s.shape[1] // chans), axis=1)
    weight_s[...] = weight_ref[layer].astype(F32).T.astype(BF16)


def updated_rows(tri_ref, z_ref, gate_ref, gain_s, weight_s):
    groups, height, nodes = tri_ref.shape
    per = height // STEP
    eight = 128 // height
    row, col = iotas(128, 128)
    wide = eight * per
    pick = (col == ((row % wide) // per) * height + (row // wide) * per + row % per).astype(BF16)
    parts = [
        dot(pick, tri_ref[q * eight : (q + 1) * eight].reshape(128, nodes))
        for q in range(groups // eight)
    ]
    rows_z = []
    for r in range(STEP):
        tri = jnp.concatenate([p[r * wide : (r + 1) * wide] for p in parts], axis=0)
        tri_norm = norm_channels(tri, gain_s[...]).astype(BF16)
        update = dot(weight_s[...], tri_norm)
        rows_z.append((z_ref[r].astype(F32) + gate_ref[r] * update).astype(BF16))
    return rows_z


def middle_kernel(
    start_ref, mask_smem, tri_ref, zin_ref, gate_ref, mask_ref, out_gain_ref, out_weight_ref, gain_ref, proj_ref,
    ab_ref, z_ref, normed_ref, out_gain_s, out_weight_s, gain_s, proj_s,
):
    step = pl.program_id(0)
    groups = ab_ref.shape[0]

    @pl.when(step == 0)
    def _():
        prepare_out(out_gain_ref, out_weight_ref, out_gain_s, out_weight_s, 0)
        prepare_in(gain_ref, proj_ref.at[1], gain_s, proj_s, 1, groups)

    rows_z = updated_rows(tri_ref, zin_ref, gate_ref, out_gain_s, out_weight_s)
    emit_factors(rows_z, step * STEP, start_ref, mask_smem, mask_ref, gain_s, proj_s, z_ref, normed_ref, ab_ref, groups)


def last_kernel(tri_ref, zin_ref, gate_ref, out_gain_ref, out_weight_ref, result_ref, out_gain_s, out_weight_s):
    @pl.when(pl.program_id(0) == 0)
    def _():
        prepare_out(out_gain_ref, out_weight_ref, out_gain_s, out_weight_s, 1)

    nodes = tri_ref.shape[2]
    ident = eye(nodes)
    for r, z in enumerate(updated_rows(tri_ref, zin_ref, gate_ref, out_gain_s, out_weight_s)):
        result_ref[r] = lax.dot_general(ident, z, NT, preferred_element_type=F32).astype(BF16)


def gate_kernel(normed_ref, weight_ref, gate_ref, *, layer):
    weight = weight_ref[layer].astype(F32).T * 0.5
    weight = weight.astype(BF16)
    for r in range(normed_ref.shape[0]):
        gate_ref[r] = jnp.tanh(dot(weight, normed_ref[r])) * 0.5 + 0.5


def triangle_kernel(ab_ref, tri_ref, sides_s, tri_s, *, layer):
    kinds, nodes, _ = sides_s.shape
    per = kinds // 2
    high = 128 // kinds
    pick = swap_matrix(128, kinds, high)
    for at in range(nodes // high):
        moved = dot(pick, ab_ref[at * 128 : (at + 1) * 128, :]).astype(BF16)
        for kind in range(kinds):
            sides_s[kind, at * high : (at + 1) * high, :] = moved[kind * high : (kind + 1) * high]
    for c in range(per):
        left, right = sides_s[c], sides_s[per + c]
        tri_s[c] = lax.dot_general(
            left, right, NT if layer == 0 else TN, preferred_element_type=F32
        ).astype(BF16)
    low = 128 // per
    back = swap_matrix(128, low, per)
    for at in range(nodes // low):
        stacked = tri_s[:, at * low : (at + 1) * low, :].reshape(128, nodes)
        tri_ref[at * 128 : (at + 1) * 128, :] = dot(back, stacked).astype(BF16)


LIMIT = 32 * 1024 * 1024


def whole(array):
    zeros = (0,) * array.ndim
    return pl.BlockSpec(array.shape, lambda i: zeros)


def body(
    pair, edge_type, node_mask, type_table, in_gain, proj_weight, gate_weight, out_gain, out_weight
):
    rows, nodes, chans = pair.shape
    hidden = out_weight.shape[1]
    groups = lax.axis_size("row")
    per = hidden // groups
    steps = rows // STEP
    start = jnp.full((1,), lax.axis_index("row") * rows, jnp.int32)
    mask = node_mask.reshape(1, nodes)
    smem = pl.BlockSpec(memory_space=pltpu.SMEM)
    params = pltpu.CompilerParams(vmem_limit_bytes=LIMIT)

    def by_row(*shape):
        return pl.BlockSpec((STEP, *shape), lambda i: (i, 0, 0))

    def by_group(height):
        return pl.BlockSpec((groups, height, nodes), lambda i: (0, i, 0))

    emitted = [
        jax.ShapeDtypeStruct((groups, rows * 2 * per, nodes), BF16),
        jax.ShapeDtypeStruct((rows, chans, nodes), BF16),
        jax.ShapeDtypeStruct((rows, chans, nodes), BF16),
    ]
    emitted_specs = [by_group(STEP * 2 * per), by_row(chans, nodes), by_row(chans, nodes)]
    gain_scratch = pltpu.VMEM((chans, nodes), F32)
    in_scratch = [gain_scratch, pltpu.VMEM((4 * hidden, chans), BF16)]
    out_scratch = [gain_scratch, pltpu.VMEM((chans, hidden), BF16)]

    def gate_of(normed, layer):
        return pl.pallas_call(
            lambda *refs: gate_kernel(*refs, layer=layer),
            out_shape=jax.ShapeDtypeStruct((rows, chans, nodes), F32),
            grid=(steps,),
            in_specs=[by_row(chans, nodes), whole(gate_weight)],
            out_specs=by_row(chans, nodes),
            compiler_params=params,
        )(normed, gate_weight)

    def triangle(ab, layer):
        sent = lax.all_to_all(ab, "row", split_axis=0, concat_axis=0, tiled=True)
        tri = pl.pallas_call(
            lambda *refs: triangle_kernel(*refs, layer=layer),
            out_shape=jax.ShapeDtypeStruct((nodes * per, nodes), BF16),
            scratch_shapes=[pltpu.VMEM((2 * per, nodes, nodes), BF16), pltpu.VMEM((per, nodes, nodes), BF16)],
            compiler_params=params,
        )(sent.reshape(nodes * 2 * per, nodes))
        return lax.all_to_all(
            tri.reshape(groups, rows * per, nodes), "row", split_axis=0, concat_axis=0, tiled=True
        )

    ab, z, normed = pl.pallas_call(
        first_kernel,
        out_shape=emitted,
        grid=(steps,),
        in_specs=[
            smem, smem, by_row(nodes, chans), whole(edge_type), whole(mask), whole(type_table), whole(in_gain),
            whole(proj_weight),
        ],
        out_specs=emitted_specs,
        scratch_shapes=in_scratch,
        compiler_params=params,
    )(start, node_mask, pair, edge_type, mask, type_table, in_gain, proj_weight)
    tri = triangle(ab, 0)
    gate = gate_of(normed, 0)
    ab, z, normed = pl.pallas_call(
        middle_kernel,
        out_shape=emitted,
        grid=(steps,),
        in_specs=[
            smem, smem, by_group(STEP * per), by_row(chans, nodes), by_row(chans, nodes), whole(mask),
            whole(out_gain), whole(out_weight), whole(in_gain), whole(proj_weight),
        ],
        out_specs=emitted_specs,
        scratch_shapes=out_scratch + in_scratch,
        compiler_params=params,
    )(start, node_mask, tri, z, gate, mask, out_gain, out_weight, in_gain, proj_weight)
    tri = triangle(ab, 1)
    gate = gate_of(normed, 1)
    return pl.pallas_call(
        last_kernel,
        out_shape=jax.ShapeDtypeStruct((rows, nodes, chans), BF16),
        grid=(steps,),
        in_specs=[
            by_group(STEP * per), by_row(chans, nodes), by_row(chans, nodes), whole(out_gain), whole(out_weight),
        ],
        out_specs=by_row(nodes, chans),
        scratch_shapes=out_scratch,
        compiler_params=params,
    )(tri, z, gate, out_gain, out_weight)


def solution(mesh):
    in_specs = (
        P(("graph", "row"), None, None),
        P(("graph", "row"), None),
        P("graph"),
        P(),
        P(),
        P(),
        P(),
        P(),
        P(),
    )
    out_specs = P(("graph", "row"), None, None)
    return jax.shard_map(body, mesh=mesh, in_specs=in_specs, out_specs=out_specs, check_vma=False)
```

```python
import jax
import jax.numpy as jnp
from jax import lax
from jax.experimental import pallas as pl
from jax.experimental.pallas import tpu as pltpu
from jax.sharding import PartitionSpec as P

F32 = jnp.float32
BF16 = jnp.bfloat16
STEP = 4
NT = (((1,), (1,)), ((), ()))
TN = (((0,), (0,)), ((), ()))


def dot(lhs, rhs):
    return jnp.dot(lhs, rhs, preferred_element_type=F32)


def iotas(rows, cols):
    return lax.broadcasted_iota(jnp.int32, (rows, cols), 0), lax.broadcasted_iota(
        jnp.int32, (rows, cols), 1
    )


def eye(n):
    row, col = iotas(n, n)
    return (row == col).astype(BF16)


def swap_matrix(n, outer, inner):
    row, col = iotas(n, n)
    return (col == (row % inner) * outer + row // inner).astype(BF16)


def norm_channels(value, gain):
    chans = value.shape[0]
    mean = jnp.sum(value, axis=0, keepdims=True) * (1.0 / chans)
    centered = value - mean
    var = jnp.sum(centered * centered, axis=0, keepdims=True) * (1.0 / chans)
    return centered * lax.rsqrt(var + 1e-05) * gain


def prepare_in(gain_ref, proj_ref, gain_s, proj_s, layer, groups):
    chans = gain_ref.shape[1]
    wide = proj_ref.shape[1]
    hidden = wide // 4
    per = hidden // groups
    gain = jnp.broadcast_to(gain_ref[layer : layer + 1, :], (chans, chans)).T
    gain_s[...] = jnp.concatenate([gain] * (gain_s.shape[1] // chans), axis=1)
    row, col = iotas(wide, wide)
    kind = row // (2 * hidden)
    group = (row // (2 * per)) % groups
    side = (row // per) % 2
    source = side * (2 * hidden) + kind * hidden + group * per + row % per
    pick = jnp.where(col == source, jnp.where(kind == 0, 0.5, 1.0), 0.0).astype(BF16)
    proj_s[...] = lax.dot_general(pick, proj_ref[...], NT, preferred_element_type=F32).astype(BF16)


def emit_factors(rows_z, first, start_ref, mask_smem, mask_ref, gain_s, proj_s, z_ref, normed_ref, ab_ref, groups):
    nodes = mask_ref.shape[0]
    lane_mask = mask_ref[...].reshape(1, nodes).astype(F32) * 0.5
    done = []
    for r, z in enumerate(rows_z):
        z_ref[r] = z
        normed = norm_channels(z.astype(F32), gain_s[...]).astype(BF16)
        normed_ref[r] = normed
        proj = dot(proj_s[...], normed)
        half = proj.shape[0] // 2
        row_mask = mask_smem[start_ref[0] + first + r].astype(F32)
        ab = (jnp.tanh(proj[:half]) + 1.0) * proj[half:] * (lane_mask * row_mask)
        done.append(ab.reshape(groups, half // groups, nodes))
        if r % 2:
            both = jnp.concatenate(done, axis=1).astype(BF16)
            height = both.shape[1]
            ab_ref[:, (r // 2) * height : (r // 2 + 1) * height, :] = both
            done = []


def first_kernel(
    start_ref, mask_smem, pair_ref, edge_ref, mask_ref, table_ref, gain_ref, proj_ref,
    ab_ref, z_ref, normed_ref, gain_s, proj_s,
):
    step = pl.program_id(0)
    groups = ab_ref.shape[0]

    @pl.when(step == 0)
    def _():
        prepare_in(gain_ref, proj_ref.at[0], gain_s, proj_s, 0, groups)

    kinds, chans = table_ref.shape
    nodes = mask_ref.shape[0]
    ident = eye(chans)
    table = table_ref[...]
    rows_z = []
    for r in range(STEP):
        edges = edge_ref[pl.ds(step * STEP + r, 1), :]
        onehot = (lax.broadcasted_iota(jnp.int32, (kinds, nodes), 0) == edges).astype(BF16)
        added = lax.dot_general(table, onehot, TN, preferred_element_type=F32)
        pair = lax.dot_general(ident, pair_ref[r], NT, preferred_element_type=F32)
        rows_z.append((pair + added).astype(BF16))
    emit_factors(rows_z, step * STEP, start_ref, mask_smem, mask_ref, gain_s, proj_s, z_ref, normed_ref, ab_ref, groups)


def prepare_out(gain_ref, weight_ref, gain_s, weight_s, layer):
    chans = gain_ref.shape[1]
    gain = jnp.broadcast_to(gain_ref[layer : layer + 1, :], (chans, chans)).T
    gain_s[...] = jnp.concatenate([gain] * (gain_s.shape[1] // chans), axis=1)
    weight_s[...] = weight_ref[layer].astype(F32).T.astype(BF16)


def updated_rows(tri_ref, z_ref, gate_ref, gain_s, weight_s):
    groups, height, nodes = tri_ref.shape
    per = height // STEP
    eight = 128 // height
    row, col = iotas(128, 128)
    wide = eight * per
    pick = (col == ((row % wide) // per) * height + (row // wide) * per + row % per).astype(BF16)
    parts = [
        dot(pick, tri_ref[q * eight : (q + 1) * eight].reshape(128, nodes))
        for q in range(groups // eight)
    ]
    rows_z = []
    for r in range(STEP):
        tri = jnp.concatenate([p[r * wide : (r + 1) * wide] for p in parts], axis=0)
        tri_norm = norm_channels(tri, gain_s[...]).astype(BF16)
        update = dot(weight_s[...], tri_norm)
        rows_z.append((z_ref[r].astype(F32) + gate_ref[r] * update).astype(BF16))
    return rows_z


def middle_kernel(
    start_ref, mask_smem, tri_ref, zin_ref, gate_ref, mask_ref, out_gain_ref, out_weight_ref, gain_ref, proj_ref,
    ab_ref, z_ref, normed_ref, out_gain_s, out_weight_s, gain_s, proj_s,
):
    step = pl.program_id(0)
    groups = ab_ref.shape[0]

    @pl.when(step == 0)
    def _():
        prepare_out(out_gain_ref, out_weight_ref, out_gain_s, out_weight_s, 0)
        prepare_in(gain_ref, proj_ref.at[1], gain_s, proj_s, 1, groups)

    rows_z = updated_rows(tri_ref, zin_ref, gate_ref, out_gain_s, out_weight_s)
    emit_factors(rows_z, step * STEP, start_ref, mask_smem, mask_ref, gain_s, proj_s, z_ref, normed_ref, ab_ref, groups)


def last_kernel(tri_ref, zin_ref, gate_ref, out_gain_ref, out_weight_ref, result_ref, out_gain_s, out_weight_s):
    @pl.when(pl.program_id(0) == 0)
    def _():
        prepare_out(out_gain_ref, out_weight_ref, out_gain_s, out_weight_s, 1)

    nodes = tri_ref.shape[2]
    ident = eye(nodes)
    for r, z in enumerate(updated_rows(tri_ref, zin_ref, gate_ref, out_gain_s, out_weight_s)):
        result_ref[r] = lax.dot_general(ident, z, NT, preferred_element_type=F32).astype(BF16)


def gate_kernel(normed_ref, weight_ref, gate_ref, *, layer):
    weight = weight_ref[layer].astype(F32).T * 0.5
    weight = weight.astype(BF16)
    for r in range(normed_ref.shape[0]):
        gate_ref[r] = jnp.tanh(dot(weight, normed_ref[r])) * 0.5 + 0.5


def triangle_kernel(ab_ref, tri_ref, sides_s, tri_s, *, layer):
    kinds, nodes, _ = sides_s.shape
    per = kinds // 2
    high = 128 // kinds
    pick = swap_matrix(128, kinds, high)
    for at in range(nodes // high):
        moved = dot(pick, ab_ref[at * 128 : (at + 1) * 128, :]).astype(BF16)
        for kind in range(kinds):
            sides_s[kind, at * high : (at + 1) * high, :] = moved[kind * high : (kind + 1) * high]
    for c in range(per):
        left, right = sides_s[c], sides_s[per + c]
        tri_s[c] = lax.dot_general(
            left, right, NT if layer == 0 else TN, preferred_element_type=F32
        ).astype(BF16)
    low = 128 // per
    back = swap_matrix(128, low, per)
    for at in range(nodes // low):
        stacked = tri_s[:, at * low : (at + 1) * low, :].reshape(128, nodes)
        tri_ref[at * 128 : (at + 1) * 128, :] = dot(back, stacked).astype(BF16)


LIMIT = 32 * 1024 * 1024


def in_hbm(array):
    return pltpu.with_memory_space_constraint(array, pltpu.HBM)


def in_vmem(array):
    return pltpu.with_memory_space_constraint(array, pltpu.VMEM)


def whole(array):
    zeros = (0,) * array.ndim
    return pl.BlockSpec(array.shape, lambda i: zeros)


def body(
    pair, edge_type, node_mask, type_table, in_gain, proj_weight, gate_weight, out_gain, out_weight
):
    rows, nodes, chans = pair.shape
    hidden = out_weight.shape[1]
    groups = lax.axis_size("row")
    per = hidden // groups
    steps = rows // STEP
    start = jnp.full((1,), lax.axis_index("row") * rows, jnp.int32)
    node_mask = in_hbm(node_mask)
    smem = pl.BlockSpec(memory_space=pltpu.SMEM)
    params = pltpu.CompilerParams(vmem_limit_bytes=LIMIT)

    def by_row(*shape):
        return pl.BlockSpec((STEP, *shape), lambda i: (i, 0, 0))

    def by_group(height):
        return pl.BlockSpec((groups, height, nodes), lambda i: (0, i, 0))

    emitted = [
        pltpu.VMEM((groups, rows * 2 * per, nodes), BF16),
        pltpu.HBM((rows, chans, nodes), BF16),
        pltpu.HBM((rows, chans, nodes), BF16),
    ]
    pair, edge_type, type_table, in_gain, proj_weight, gate_weight, out_gain, out_weight = (
        in_hbm(x)
        for x in (pair, edge_type, type_table, in_gain, proj_weight, gate_weight, out_gain, out_weight)
    )
    emitted_specs = [by_group(STEP * 2 * per), by_row(chans, nodes), by_row(chans, nodes)]
    gain_scratch = pltpu.VMEM((chans, nodes), F32)
    in_scratch = [gain_scratch, pltpu.VMEM((4 * hidden, chans), BF16)]
    out_scratch = [gain_scratch, pltpu.VMEM((chans, hidden), BF16)]

    def gate_of(normed, layer):
        return pl.pallas_call(
            lambda *refs: gate_kernel(*refs, layer=layer),
            out_shape=pltpu.HBM((rows, chans, nodes), F32),
            grid=(steps,),
            in_specs=[by_row(chans, nodes), whole(gate_weight)],
            out_specs=by_row(chans, nodes),
            compiler_params=params,
        )(in_hbm(normed), gate_weight)

    def triangle(ab, layer):
        sent = lax.all_to_all(ab, "row", split_axis=0, concat_axis=0, tiled=True)
        tri = pl.pallas_call(
            lambda *refs: triangle_kernel(*refs, layer=layer),
            out_shape=pltpu.HBM((nodes * per, nodes), BF16),
            scratch_shapes=[pltpu.VMEM((2 * per, nodes, nodes), BF16), pltpu.VMEM((per, nodes, nodes), BF16)],
            compiler_params=params,
        )(in_vmem(sent.reshape(nodes * 2 * per, nodes)))
        return lax.all_to_all(
            tri.reshape(groups, rows * per, nodes), "row", split_axis=0, concat_axis=0, tiled=True
        )

    ab, z, normed = pl.pallas_call(
        first_kernel,
        out_shape=emitted,
        grid=(steps,),
        in_specs=[
            smem, smem, by_row(nodes, chans), whole(edge_type), whole(node_mask), whole(type_table), whole(in_gain),
            whole(proj_weight),
        ],
        out_specs=emitted_specs,
        scratch_shapes=in_scratch,
        compiler_params=params,
    )(start, node_mask, pair, edge_type, node_mask, type_table, in_gain, proj_weight)
    tri = triangle(ab, 0)
    gate = gate_of(normed, 0)
    ab, z, normed = pl.pallas_call(
        middle_kernel,
        out_shape=emitted,
        grid=(steps,),
        in_specs=[
            smem, smem, by_group(STEP * per), by_row(chans, nodes), by_row(chans, nodes), whole(node_mask),
            whole(out_gain), whole(out_weight), whole(in_gain), whole(proj_weight),
        ],
        out_specs=emitted_specs,
        scratch_shapes=out_scratch + in_scratch,
        compiler_params=params,
    )(start, node_mask, in_vmem(tri), in_hbm(z), in_hbm(gate), node_mask, out_gain, out_weight, in_gain, proj_weight)
    tri = triangle(ab, 1)
    gate = gate_of(normed, 1)
    return pl.pallas_call(
        last_kernel,
        out_shape=jax.ShapeDtypeStruct((rows, nodes, chans), BF16),
        grid=(steps,),
        in_specs=[
            by_group(STEP * per), by_row(chans, nodes), by_row(chans, nodes), whole(out_gain), whole(out_weight),
        ],
        out_specs=by_row(nodes, chans),
        scratch_shapes=out_scratch,
        compiler_params=params,
    )(in_vmem(tri), in_hbm(z), in_hbm(gate), out_gain, out_weight)


def solution(mesh):
    in_specs = (
        P(("graph", "row"), None, None),
        P(("graph", "row"), None),
        P("graph"),
        P(),
        P(),
        P(),
        P(),
        P(),
        P(),
    )
    out_specs = P(("graph", "row"), None, None)
    return jax.shard_map(body, mesh=mesh, in_specs=in_specs, out_specs=out_specs, check_vma=False)
```

```python
import jax
import jax.numpy as jnp
from jax import lax
from jax.experimental import pallas as pl
from jax.experimental.pallas import tpu as pltpu
from jax.sharding import PartitionSpec as P

F32 = jnp.float32
BF16 = jnp.bfloat16
STEP = 4
NT = (((1,), (1,)), ((), ()))
TN = (((0,), (0,)), ((), ()))


def dot(lhs, rhs):
    return jnp.dot(lhs, rhs, preferred_element_type=F32)


def iotas(rows, cols):
    return lax.broadcasted_iota(jnp.int32, (rows, cols), 0), lax.broadcasted_iota(
        jnp.int32, (rows, cols), 1
    )


def eye(n):
    row, col = iotas(n, n)
    return (row == col).astype(BF16)


def swap_matrix(n, outer, inner):
    row, col = iotas(n, n)
    return (col == (row % inner) * outer + row // inner).astype(BF16)


def norm_channels(value, gain):
    chans = value.shape[0]
    mean = jnp.sum(value, axis=0, keepdims=True) * (1.0 / chans)
    centered = value - mean
    var = jnp.sum(centered * centered, axis=0, keepdims=True) * (1.0 / chans)
    return centered * lax.rsqrt(var + 1e-05) * gain


def prepare_in(gain_ref, proj_ref, weight_ref, gain_s, proj_s, layer, groups):
    chans = gain_ref.shape[1]
    wide = proj_ref.shape[1]
    hidden = wide // 4
    per = hidden // groups
    gain = jnp.broadcast_to(gain_ref[layer : layer + 1, :], (chans, chans)).T
    gain_s[...] = jnp.concatenate([gain] * (gain_s.shape[1] // chans), axis=1)
    row, col = iotas(2 * hidden, hidden)
    place = col // per * (2 * per) + col % per
    picks = [(row == place + side * per).astype(BF16) for side in range(2)]
    for kind in range(2):
        rows = sum(
            lax.dot_general(
                picks[side], proj_ref[:, (2 * side + kind) * hidden : (2 * side + kind + 1) * hidden], NT,
                preferred_element_type=F32,
            )
            for side in range(2)
        )
        proj_s[2 * kind * hidden : 2 * (kind + 1) * hidden] = (rows * (1.0 - 0.5 * (1 - kind))).astype(BF16)
    proj_s[wide:] = (weight_ref[...].astype(F32).T * 0.5).astype(BF16)


def emit_factors(rows_z, first, own_mask, lane_mask, gain_s, proj_s, ab_ref, z_ref, gate_ref, groups):
    nodes = lane_mask.shape[1]
    done = []
    for r, z in enumerate(rows_z):
        normed = norm_channels(z.astype(F32), gain_s[...]).astype(BF16)
        proj = dot(proj_s[...], normed)
        half = ab_ref.shape[1] // z_ref.shape[0] * groups
        row = first + r
        z_ref[row] = z
        gate_ref[row] = jnp.tanh(proj[2 * half :]) * 0.5 + 0.5
        ab = (jnp.tanh(proj[:half]) + 1.0) * proj[half : 2 * half] * (lane_mask * own_mask[row : row + 1])
        done.append(ab.reshape(groups, half // groups, nodes))
        if r % 2:
            both = jnp.concatenate(done, axis=1).astype(BF16)
            height = both.shape[1]
            ab_ref[:, row // 2 * height : (row // 2 + 1) * height, :] = both
            done = []


def start_all(pairs, sems):
    copies = [pltpu.make_async_copy(source, target, sems.at[i]) for i, (source, target) in enumerate(pairs)]
    for copy in copies:
        copy.start()
    return copies


def chunk(ref, at):
    return ref.at[pl.ds(at * STEP, STEP)]


def row_masks(mask_ref, rows):
    nodes = mask_ref.shape[0]
    lanes = mask_ref[...].reshape(1, nodes).astype(F32)
    row, col = iotas(16, nodes)
    own = jnp.where(col == lax.axis_index("row") * rows + row, lanes, 0.0)
    return jnp.sum(own, axis=1, keepdims=True), lanes * 0.5


def embedded_rows(step, pair_ref, edge_ref, table_ref):
    kinds, chans = table_ref.shape
    nodes = edge_ref.shape[1]
    ident = eye(chans)
    table = table_ref[...]
    rows_z = []
    for r in range(STEP):
        edges = edge_ref[pl.ds(step * STEP + r, 1), :]
        onehot = (lax.broadcasted_iota(jnp.int32, (kinds, nodes), 0) == edges).astype(BF16)
        added = lax.dot_general(table, onehot, TN, preferred_element_type=F32)
        pair = lax.dot_general(ident, pair_ref[r], NT, preferred_element_type=F32)
        rows_z.append((pair + added).astype(BF16))
    return rows_z


def first_kernel(
    pair_hbm, edge_hbm, mask_hbm, table_hbm, gain_hbm, proj_hbm, weight_hbm,
    ab_ref, z_ref, gate_ref,
    pair_ref, edge_ref, mask_ref, table_ref, gain_ref, proj_ref, weight_ref, gain_s, proj_s, sems,
):
    rows, groups = pair_ref.shape[0], ab_ref.shape[0]
    small = [(gain_hbm, gain_ref), (proj_hbm.at[0], proj_ref), (weight_hbm.at[0], weight_ref), (table_hbm, table_ref), (mask_hbm, mask_ref), (edge_hbm, edge_ref)]
    large = [(chunk(pair_hbm, at), chunk(pair_ref, at)) for at in range(rows // STEP)]
    copies = start_all(small + large, sems)
    for copy in copies[:6]:
        copy.wait()
    prepare_in(gain_ref, proj_ref, weight_ref, gain_s, proj_s, 0, groups)
    own_mask, lane_mask = row_masks(mask_ref, rows)
    for at in range(rows // STEP):
        copies[6 + at].wait()
        rows_z = embedded_rows(at, chunk(pair_ref, at), edge_ref, table_ref)
        emit_factors(rows_z, at * STEP, own_mask, lane_mask, gain_s, proj_s, ab_ref, z_ref, gate_ref, groups)


def prepare_out(gain_ref, weight_ref, gain_s, weight_s, layer):
    chans = gain_ref.shape[1]
    gain = jnp.broadcast_to(gain_ref[layer : layer + 1, :], (chans, chans)).T
    gain_s[...] = jnp.concatenate([gain] * (gain_s.shape[1] // chans), axis=1)
    weight_s[...] = weight_ref[...].astype(F32).T.astype(BF16)


def products_of(tri_ref, at):
    groups, _, nodes = tri_ref.shape
    height = STEP * 4
    per = 128 // groups
    eight = 128 // height
    row, col = iotas(128, 128)
    wide = eight * per
    pick = (col == ((row % wide) // per) * height + (row // wide) * per + row % per).astype(BF16)
    parts = [
        dot(pick, tri_ref[q * eight : (q + 1) * eight, at * height : (at + 1) * height, :].reshape(128, nodes))
        for q in range(groups // eight)
    ]
    return [
        jnp.concatenate([p[r * wide : (r + 1) * wide] for p in parts], axis=0) for r in range(STEP)
    ]


def updated_rows(products, z_ref, gate_ref, gain_s, weight_s):
    rows_z = []
    for r, tri in enumerate(products):
        tri_norm = norm_channels(tri, gain_s[...]).astype(BF16)
        update = dot(weight_s[...], tri_norm)
        rows_z.append((z_ref[r].astype(F32) + gate_ref[r].astype(F32) * update).astype(BF16))
    return rows_z


def middle_kernel(
    tri_ref, zin_ref, gin_ref, mask_hbm, out_gain_hbm, out_weight_hbm, gain_hbm, proj_hbm, weight_hbm,
    ab_ref, z_ref, gate_ref,
    mask_ref, out_gain_ref, out_weight_ref, gain_ref, proj_ref, weight_ref,
    out_gain_s, out_weight_s, gain_s, proj_s, sems,
):
    rows, groups = zin_ref.shape[0], ab_ref.shape[0]
    copies = start_all(
        [
            (out_gain_hbm, out_gain_ref), (out_weight_hbm.at[0], out_weight_ref), (gain_hbm, gain_ref),
            (proj_hbm.at[1], proj_ref), (weight_hbm.at[1], weight_ref), (mask_hbm, mask_ref),
        ],
        sems,
    )
    products = products_of(tri_ref, 0)
    for copy in copies:
        copy.wait()
    prepare_out(out_gain_ref, out_weight_ref, out_gain_s, out_weight_s, 0)
    prepare_in(gain_ref, proj_ref, weight_ref, gain_s, proj_s, 1, groups)
    own_mask, lane_mask = row_masks(mask_ref, rows)
    for at in range(rows // STEP):
        if at:
            products = products_of(tri_ref, at)
        rows_z = updated_rows(products, chunk(zin_ref, at), chunk(gin_ref, at), out_gain_s, out_weight_s)
        emit_factors(rows_z, at * STEP, own_mask, lane_mask, gain_s, proj_s, ab_ref, z_ref, gate_ref, groups)


def last_kernel(
    tri_ref, z_ref, gate_ref, out_gain_hbm, out_weight_hbm, result_hbm,
    out_gain_ref, out_weight_ref, result_ref, out_gain_s, out_weight_s, sems, out_sems,
):
    rows = z_ref.shape[0]
    copies = start_all([(out_gain_hbm, out_gain_ref), (out_weight_hbm.at[1], out_weight_ref)], sems)
    products = products_of(tri_ref, 0)
    for copy in copies:
        copy.wait()
    prepare_out(out_gain_ref, out_weight_ref, out_gain_s, out_weight_s, 1)
    ident = eye(tri_ref.shape[2])
    sent = []
    for at in range(rows // STEP):
        if at:
            products = products_of(tri_ref, at)
        rows_z = updated_rows(products, chunk(z_ref, at), chunk(gate_ref, at), out_gain_s, out_weight_s)
        for r, z in enumerate(rows_z):
            result_ref[at * STEP + r] = lax.dot_general(ident, z, NT, preferred_element_type=F32).astype(BF16)
        copy = pltpu.make_async_copy(chunk(result_ref, at), chunk(result_hbm, at), out_sems.at[at])
        copy.start()
        sent.append(copy)
    for copy in sent:
        copy.wait()


def triangle_kernel(ab_ref, tri_ref, sides_s, tri_s, *, layer):
    kinds, nodes, _ = sides_s.shape
    per = kinds // 2
    high = 128 // kinds
    pick = swap_matrix(128, kinds, high)
    for at in range(nodes // high):
        moved = dot(pick, ab_ref[at * 128 : (at + 1) * 128, :]).astype(BF16)
        for kind in range(kinds):
            sides_s[kind, at * high : (at + 1) * high, :] = moved[kind * high : (kind + 1) * high]
    for c in range(per):
        left, right = sides_s[c], sides_s[per + c]
        tri_s[c] = lax.dot_general(
            left, right, NT if layer == 0 else TN, preferred_element_type=F32
        ).astype(BF16)
    low = 128 // per
    back = swap_matrix(128, low, per)
    for at in range(nodes // low):
        stacked = tri_s[:, at * low : (at + 1) * low, :].reshape(128, nodes)
        tri_ref[at * 128 : (at + 1) * 128, :] = dot(back, stacked).astype(BF16)


LIMIT = 32 * 1024 * 1024


def in_hbm(array):
    return pltpu.with_memory_space_constraint(array, pltpu.HBM)


def in_vmem(array):
    return pltpu.with_memory_space_constraint(array, pltpu.VMEM)


def whole(array):
    zeros = (0,) * array.ndim
    return pl.BlockSpec(array.shape, lambda i: zeros)


def body(
    pair, edge_type, node_mask, type_table, in_gain, proj_weight, gate_weight, out_gain, out_weight
):
    rows, nodes, chans = pair.shape
    hidden = out_weight.shape[1]
    groups = lax.axis_size("row")
    per = hidden // groups
    steps = rows // STEP
    node_mask = in_hbm(node_mask)
    params = pltpu.CompilerParams(vmem_limit_bytes=LIMIT)

    def by_row(*shape):
        return pl.BlockSpec((STEP, *shape), lambda i: (i, 0, 0))

    anywhere = pl.BlockSpec(memory_space=pl.ANY)
    vmem = pl.BlockSpec(memory_space=pltpu.VMEM)
    factors = pltpu.VMEM((groups, rows * 2 * per, nodes), BF16)
    emitted = [factors, pltpu.VMEM((rows, chans, nodes), BF16), pltpu.VMEM((rows, chans, nodes), F32)]
    pair, edge_type, type_table, in_gain, proj_weight, gate_weight, out_gain, out_weight = (
        in_hbm(x)
        for x in (pair, edge_type, type_table, in_gain, proj_weight, gate_weight, out_gain, out_weight)
    )
    gain_scratch = pltpu.VMEM((chans, nodes), F32)
    in_scratch = [gain_scratch, pltpu.VMEM((4 * hidden + chans, chans), BF16)]
    out_scratch = [gain_scratch, pltpu.VMEM((chans, hidden), BF16)]
    gains = pltpu.VMEM(in_gain.shape, F32)
    proj_buffer = pltpu.VMEM((chans, 4 * hidden), BF16)
    out_buffer = pltpu.VMEM((hidden, chans), BF16)
    mask_buffer = pltpu.VMEM((nodes,), jnp.int32)

    def sems(count):
        return pltpu.SemaphoreType.DMA((count,))

    def triangle(ab, layer):
        sent = lax.all_to_all(ab, "row", split_axis=0, concat_axis=0, tiled=True)
        tri = pl.pallas_call(
            lambda *refs: triangle_kernel(*refs, layer=layer),
            out_shape=pltpu.VMEM((nodes * per, nodes), BF16),
            in_specs=[vmem],
            out_specs=vmem,
            scratch_shapes=[pltpu.VMEM((2 * per, nodes, nodes), BF16), pltpu.VMEM((per, nodes, nodes), BF16)],
            compiler_params=params,
        )(in_vmem(sent.reshape(nodes * 2 * per, nodes)))
        return lax.all_to_all(
            tri.reshape(groups, rows * per, nodes), "row", split_axis=0, concat_axis=0, tiled=True
        )

    ab, z, gate = pl.pallas_call(
        first_kernel,
        out_shape=emitted,
        in_specs=[anywhere] * 7,
        out_specs=[vmem] * 3,
        scratch_shapes=[
            pltpu.VMEM(pair.shape, BF16), pltpu.VMEM(edge_type.shape, jnp.int32), mask_buffer,
            pltpu.VMEM(type_table.shape, BF16), gains, proj_buffer, out_buffer, *in_scratch, sems(6 + steps),
        ],
        compiler_params=params,
    )(pair, edge_type, node_mask, type_table, in_gain, proj_weight, gate_weight)
    tri = triangle(ab, 0)
    ab, z, gate = pl.pallas_call(
        middle_kernel,
        out_shape=emitted,
        in_specs=[vmem] * 3 + [anywhere] * 6,
        out_specs=[vmem] * 3,
        scratch_shapes=[
            mask_buffer, gains, out_buffer, gains, proj_buffer, out_buffer, *out_scratch, *in_scratch, sems(6),
        ],
        compiler_params=params,
    )(in_vmem(tri), in_vmem(z), in_vmem(gate), node_mask, out_gain, out_weight, in_gain, proj_weight, gate_weight)
    tri = triangle(ab, 1)
    return pl.pallas_call(
        last_kernel,
        out_shape=pltpu.HBM((rows, nodes, chans), BF16),
        in_specs=[vmem] * 3 + [anywhere] * 2,
        out_specs=anywhere,
        scratch_shapes=[
            gains, out_buffer, pltpu.VMEM((rows, nodes, chans), BF16), *out_scratch, sems(2), sems(steps),
        ],
        compiler_params=params,
    )(in_vmem(tri), in_vmem(z), in_vmem(gate), out_gain, out_weight)


def solution(mesh):
    in_specs = (
        P(("graph", "row"), None, None),
        P(("graph", "row"), None),
        P("graph"),
        P(),
        P(),
        P(),
        P(),
        P(),
        P(),
    )
    out_specs = P(("graph", "row"), None, None)
    return jax.shard_map(body, mesh=mesh, in_specs=in_specs, out_specs=out_specs, check_vma=False)
```

```python
import jax
import jax.numpy as jnp
from jax import lax
from jax.experimental import pallas as pl
from jax.experimental.pallas import tpu as pltpu
from jax.sharding import PartitionSpec as P

F32 = jnp.float32
BF16 = jnp.bfloat16
STEP = 4
NT = (((1,), (1,)), ((), ()))
TN = (((0,), (0,)), ((), ()))


def dot(lhs, rhs):
    return jnp.dot(lhs, rhs, preferred_element_type=F32)


def iotas(rows, cols):
    return lax.broadcasted_iota(jnp.int32, (rows, cols), 0), lax.broadcasted_iota(
        jnp.int32, (rows, cols), 1
    )


def eye(n):
    row, col = iotas(n, n)
    return (row == col).astype(BF16)


def swap_matrix(n, outer, inner):
    row, col = iotas(n, n)
    return (col == (row % inner) * outer + row // inner).astype(BF16)


def norm_channels(value, gain):
    chans = value.shape[0]
    mean = jnp.sum(value, axis=0, keepdims=True) * (1.0 / chans)
    centered = value - mean
    var = jnp.sum(centered * centered, axis=0, keepdims=True) * (1.0 / chans)
    return centered * lax.rsqrt(var + 1e-05) * gain


def prepare_in(gain_ref, proj_ref, weight_ref, gain_s, proj_s, layer, groups):
    chans = gain_ref.shape[1]
    wide = proj_ref.shape[1]
    hidden = wide // 4
    per = hidden // groups
    gain = jnp.broadcast_to(gain_ref[layer : layer + 1, :], (chans, chans)).T
    gain_s[...] = jnp.concatenate([gain] * (gain_s.shape[1] // chans), axis=1)
    row, col = iotas(2 * hidden, hidden)
    place = col // per * (2 * per) + col % per
    picks = [(row == place + side * per).astype(BF16) for side in range(2)]
    for kind in range(2):
        rows = sum(
            lax.dot_general(
                picks[side], proj_ref[:, (2 * side + kind) * hidden : (2 * side + kind + 1) * hidden], NT,
                preferred_element_type=F32,
            )
            for side in range(2)
        )
        proj_s[2 * kind * hidden : 2 * (kind + 1) * hidden] = (rows * (1.0 - 0.5 * (1 - kind))).astype(BF16)
    proj_s[wide:] = (weight_ref[...].astype(F32).T * 0.5).astype(BF16)


def emit_factors(rows_z, first, pair_mask_s, gain_s, proj_s, ab_ref, z_ref, gate_ref, groups):
    nodes = pair_mask_s.shape[1]
    half = ab_ref.shape[1] // z_ref.shape[0] * groups
    for r in range(0, len(rows_z), 2):
        normed = [norm_channels(z.astype(F32), gain_s[...]).astype(BF16) for z in rows_z[r : r + 2]]
        both_rows = dot(proj_s[...], jnp.concatenate(normed, axis=1))
        done = []
        for i in range(2):
            row = first + r + i
            proj = both_rows[:, i * nodes : (i + 1) * nodes]
            z_ref[row] = rows_z[r + i]
            gate_ref[row] = jnp.tanh(proj[2 * half :]) * 0.5 + 0.5
            ab = (jnp.tanh(proj[:half]) + 1.0) * proj[half : 2 * half] * pair_mask_s[row : row + 1, :]
            done.append(ab.reshape(groups, half // groups, nodes))
        both = jnp.concatenate(done, axis=1).astype(BF16)
        height = both.shape[1]
        at = (first + r) // 2 * height
        ab_ref[:, at : at + height, :] = both


def start_all(pairs, sems):
    copies = [pltpu.make_async_copy(source, target, sems.at[i]) for i, (source, target) in enumerate(pairs)]
    for copy in copies:
        copy.start()
    return copies


def chunk(ref, at):
    return ref.at[pl.ds(at * STEP, STEP)]


def row_masks(mask_ref, rows):
    nodes = mask_ref.shape[0]
    lanes = mask_ref[...].reshape(1, nodes).astype(F32)
    row, col = iotas(16, nodes)
    own = jnp.where(col == lax.axis_index("row") * rows + row, lanes, 0.0)
    return jnp.sum(own, axis=1, keepdims=True) * (lanes * 0.5)


def embedded_rows(step, pair_ref, edge_ref, table_ref):
    kinds, chans = table_ref.shape
    nodes = edge_ref.shape[1]
    ident = eye(chans)
    table = table_ref[...]
    rows_z = []
    for r in range(0, STEP, 2):
        edges = jnp.concatenate([edge_ref[pl.ds(step * STEP + r + i, 1), :] for i in range(2)], axis=1)
        onehot = (lax.broadcasted_iota(jnp.int32, (kinds, 2 * nodes), 0) == edges).astype(BF16)
        added = lax.dot_general(table, onehot, TN, preferred_element_type=F32)
        pair = lax.dot_general(
            ident, pair_ref[r : r + 2].reshape(2 * nodes, chans), NT, preferred_element_type=F32
        )
        z = (pair + added).astype(BF16)
        rows_z += [z[:, :nodes], z[:, nodes:]]
    return rows_z


def first_kernel(
    pair_hbm, edge_hbm, mask_hbm, table_hbm, gain_hbm, proj_hbm, weight_hbm, out_gain_hbm, out_weight_hbm,
    ab_ref, z_ref, gate_ref, gain_s, proj_s, pair_mask_s, out_gain_s, out_weight_s,
    pair_ref, edge_ref, mask_ref, table_ref, gain_ref, proj_ref, weight_ref, out_gain_ref, out_weight_ref, sems,
):
    rows, groups = pair_ref.shape[0], ab_ref.shape[0]
    small = [
        (gain_hbm, gain_ref), (proj_hbm, proj_ref), (weight_hbm, weight_ref), (table_hbm, table_ref),
        (mask_hbm, mask_ref), (edge_hbm, edge_ref), (out_gain_hbm, out_gain_ref), (out_weight_hbm, out_weight_ref),
    ]
    large = [(chunk(pair_hbm, at), chunk(pair_ref, at)) for at in range(rows // STEP)]
    copies = start_all(small + large, sems)
    for copy in copies[: len(small)]:
        copy.wait()
    for layer in range(2):
        prepare_in(
            gain_ref, proj_ref.at[layer], weight_ref.at[layer], gain_s.at[layer], proj_s.at[layer], layer, groups
        )
        prepare_out(out_gain_ref, out_weight_ref.at[layer], out_gain_s.at[layer], out_weight_s.at[layer], layer)
    pair_mask_s[...] = row_masks(mask_ref, rows)
    for at in range(rows // STEP):
        copies[len(small) + at].wait()
        rows_z = embedded_rows(at, chunk(pair_ref, at), edge_ref, table_ref)
        emit_factors(rows_z, at * STEP, pair_mask_s, gain_s.at[0], proj_s.at[0], ab_ref, z_ref, gate_ref, groups)


def prepare_out(gain_ref, weight_ref, gain_s, weight_s, layer):
    chans = gain_ref.shape[1]
    gain = jnp.broadcast_to(gain_ref[layer : layer + 1, :], (chans, chans)).T
    gain_s[...] = jnp.concatenate([gain] * (gain_s.shape[1] // chans), axis=1)
    weight_s[...] = weight_ref[...].astype(F32).T.astype(BF16)


def products_of(tri_ref, at):
    groups, _, nodes = tri_ref.shape
    height = STEP * 4
    per = 128 // groups
    eight = 128 // height
    row, col = iotas(128, 128)
    wide = eight * per
    pick = (col == ((row % wide) // per) * height + (row // wide) * per + row % per).astype(BF16)
    blocks = [
        tri_ref[q * eight : (q + 1) * eight, at * height : (at + 1) * height, :].reshape(128, nodes)
        for q in range(groups // eight)
    ]
    parts = []
    for q in range(0, groups // eight, 2):
        moved = dot(pick, jnp.concatenate(blocks[q : q + 2], axis=1))
        parts += [moved[:, :nodes], moved[:, nodes:]]
    return [
        jnp.concatenate([p[r * wide : (r + 1) * wide] for p in parts], axis=0) for r in range(STEP)
    ]


def updated_rows(products, z_ref, gate_ref, gain_s, weight_s):
    rows_z = []
    nodes = z_ref.shape[2]
    for r in range(0, STEP, 2):
        tri_norm = [norm_channels(tri, gain_s[...]).astype(BF16) for tri in products[r : r + 2]]
        update = dot(weight_s[...], jnp.concatenate(tri_norm, axis=1))
        for i in range(2):
            rows_z.append(
                (z_ref[r + i].astype(F32) + gate_ref[r + i] * update[:, i * nodes : (i + 1) * nodes]).astype(BF16)
            )
    return rows_z


def middle_kernel(
    tri_ref, zin_ref, gin_ref, gain_s, proj_s, pair_mask_s, out_gain_s, out_weight_s, ab_ref, z_ref, gate_ref
):
    rows, groups = zin_ref.shape[0], ab_ref.shape[0]
    for at in range(rows // STEP):
        rows_z = updated_rows(
            products_of(tri_ref, at), chunk(zin_ref, at), chunk(gin_ref, at), out_gain_s.at[0], out_weight_s.at[0]
        )
        emit_factors(rows_z, at * STEP, pair_mask_s, gain_s.at[1], proj_s.at[1], ab_ref, z_ref, gate_ref, groups)


def last_kernel(tri_ref, z_ref, gate_ref, out_gain_s, out_weight_s, result_hbm, result_ref, out_sems):
    rows = z_ref.shape[0]
    ident = eye(tri_ref.shape[2])
    sent = []
    for at in range(rows // STEP):
        rows_z = updated_rows(
            products_of(tri_ref, at), chunk(z_ref, at), chunk(gate_ref, at), out_gain_s.at[1], out_weight_s.at[1]
        )
        for r in range(0, STEP, 2):
            turned = lax.dot_general(
                ident, jnp.concatenate(rows_z[r : r + 2], axis=0), NT, preferred_element_type=F32
            ).astype(BF16)
            chans = turned.shape[1] // 2
            result_ref[at * STEP + r] = turned[:, :chans]
            result_ref[at * STEP + r + 1] = turned[:, chans:]
        copy = pltpu.make_async_copy(chunk(result_ref, at), chunk(result_hbm, at), out_sems.at[at])
        copy.start()
        sent.append(copy)
    for copy in sent:
        copy.wait()


def triangle_kernel(ab_ref, tri_ref, sides_s, tri_s, *, layer):
    kinds, nodes, _ = sides_s.shape
    per = kinds // 2
    high = 128 // kinds
    pick = swap_matrix(128, kinds, high)
    for at in range(nodes // high):
        moved = dot(pick, ab_ref[at * 128 : (at + 1) * 128, :]).astype(BF16)
        for kind in range(kinds):
            sides_s[kind, at * high : (at + 1) * high, :] = moved[kind * high : (kind + 1) * high]
    for c in range(per):
        left, right = sides_s[c], sides_s[per + c]
        tri_s[c] = lax.dot_general(
            left, right, NT if layer == 0 else TN, preferred_element_type=F32
        ).astype(BF16)
    low = 128 // per
    back = swap_matrix(128, low, per)
    for at in range(nodes // low):
        stacked = tri_s[:, at * low : (at + 1) * low, :].reshape(128, nodes)
        tri_ref[at * 128 : (at + 1) * 128, :] = dot(back, stacked).astype(BF16)


LIMIT = 32 * 1024 * 1024


def in_hbm(array):
    return pltpu.with_memory_space_constraint(array, pltpu.HBM)


def in_vmem(array):
    return pltpu.with_memory_space_constraint(array, pltpu.VMEM)


def whole(array):
    zeros = (0,) * array.ndim
    return pl.BlockSpec(array.shape, lambda i: zeros)


def body(
    pair, edge_type, node_mask, type_table, in_gain, proj_weight, gate_weight, out_gain, out_weight
):
    rows, nodes, chans = pair.shape
    hidden = out_weight.shape[1]
    groups = lax.axis_size("row")
    per = hidden // groups
    steps = rows // STEP
    node_mask = in_hbm(node_mask)
    params = pltpu.CompilerParams(vmem_limit_bytes=LIMIT)

    def by_row(*shape):
        return pl.BlockSpec((STEP, *shape), lambda i: (i, 0, 0))

    anywhere = pl.BlockSpec(memory_space=pl.ANY)
    vmem = pl.BlockSpec(memory_space=pltpu.VMEM)
    factors = pltpu.VMEM((groups, rows * 2 * per, nodes), BF16)
    emitted = [factors, pltpu.VMEM((rows, chans, nodes), BF16), pltpu.VMEM((rows, chans, nodes), F32)]
    pair, edge_type, type_table, in_gain, proj_weight, gate_weight, out_gain, out_weight = (
        in_hbm(x)
        for x in (pair, edge_type, type_table, in_gain, proj_weight, gate_weight, out_gain, out_weight)
    )
    prepared = [
        pltpu.VMEM((2, chans, nodes), F32), pltpu.VMEM((2, 4 * hidden + chans, chans), BF16),
        pltpu.VMEM((16, nodes), F32), pltpu.VMEM((2, hidden, nodes), F32), pltpu.VMEM((2, chans, hidden), BF16),
    ]

    def sems(count):
        return pltpu.SemaphoreType.DMA((count,))

    def triangle(ab, layer):
        sent = lax.all_to_all(ab, "row", split_axis=0, concat_axis=0, tiled=True)
        tri = pl.pallas_call(
            lambda *refs: triangle_kernel(*refs, layer=layer),
            out_shape=pltpu.VMEM((nodes * per, nodes), BF16),
            in_specs=[vmem],
            out_specs=vmem,
            scratch_shapes=[pltpu.VMEM((2 * per, nodes, nodes), BF16), pltpu.VMEM((per, nodes, nodes), BF16)],
            compiler_params=params,
        )(in_vmem(sent.reshape(nodes * 2 * per, nodes)))
        return lax.all_to_all(
            tri.reshape(groups, rows * per, nodes), "row", split_axis=0, concat_axis=0, tiled=True
        )

    arguments = (
        pair, edge_type, node_mask, type_table, in_gain, proj_weight, gate_weight, out_gain, out_weight
    )
    ab, z, gate, *weights = pl.pallas_call(
        first_kernel,
        out_shape=emitted + prepared,
        in_specs=[anywhere] * 9,
        out_specs=[vmem] * 8,
        scratch_shapes=[*(pltpu.VMEM(x.shape, x.dtype) for x in arguments), sems(8 + steps)],
        compiler_params=params,
    )(*arguments)
    weights = [in_vmem(x) for x in weights]
    tri = triangle(ab, 0)
    ab, z, gate = pl.pallas_call(
        middle_kernel,
        out_shape=emitted,
        in_specs=[vmem] * 8,
        out_specs=[vmem] * 3,
        compiler_params=params,
    )(in_vmem(tri), in_vmem(z), in_vmem(gate), *weights)
    tri = triangle(ab, 1)
    return pl.pallas_call(
        last_kernel,
        out_shape=pltpu.HBM((rows, nodes, chans), BF16),
        in_specs=[vmem] * 5,
        out_specs=anywhere,
        scratch_shapes=[pltpu.VMEM((rows, nodes, chans), BF16), sems(steps)],
        compiler_params=params,
    )(in_vmem(tri), in_vmem(z), in_vmem(gate), *weights[3:])


def solution(mesh):
    in_specs = (
        P(("graph", "row"), None, None),
        P(("graph", "row"), None),
        P("graph"),
        P(),
        P(),
        P(),
        P(),
        P(),
        P(),
    )
    out_specs = P(("graph", "row"), None, None)
    return jax.shard_map(body, mesh=mesh, in_specs=in_specs, out_specs=out_specs, check_vma=False)
```

```python
import jax
import jax.numpy as jnp
from jax import lax
from jax.experimental import pallas as pl
from jax.experimental.pallas import tpu as pltpu
from jax.sharding import PartitionSpec as P

F32 = jnp.float32
BF16 = jnp.bfloat16
STEP = 4
NT = (((1,), (1,)), ((), ()))
TN = (((0,), (0,)), ((), ()))


def dot(lhs, rhs):
    return jnp.dot(lhs, rhs, preferred_element_type=F32)


def iotas(rows, cols):
    return lax.broadcasted_iota(jnp.int32, (rows, cols), 0), lax.broadcasted_iota(
        jnp.int32, (rows, cols), 1
    )


def eye(n):
    row, col = iotas(n, n)
    return (row == col).astype(BF16)


def swap_matrix(n, outer, inner):
    row, col = iotas(n, n)
    return (col == (row % inner) * outer + row // inner).astype(BF16)


def norm_channels(value, gain):
    chans = value.shape[0]
    mean = jnp.sum(value, axis=0, keepdims=True) * (1.0 / chans)
    centered = value - mean
    var = jnp.sum(centered * centered, axis=0, keepdims=True) * (1.0 / chans)
    return centered * lax.rsqrt(var + 1e-05) * gain


def prepare_in(gain_ref, proj_ref, weight_ref, gain_s, proj_s, layer, groups):
    chans = gain_ref.shape[1]
    wide = proj_ref.shape[1]
    hidden = wide // 4
    per = hidden // groups
    gain = jnp.broadcast_to(gain_ref[layer : layer + 1, :], (chans, chans)).T
    gain_s[...] = jnp.concatenate([gain] * (gain_s.shape[1] // chans), axis=1)
    row, col = iotas(2 * hidden, hidden)
    place = col // per * (2 * per) + col % per
    picks = [(row == place + side * per).astype(BF16) for side in range(2)]
    for kind in range(2):
        rows = sum(
            lax.dot_general(
                picks[side], proj_ref[:, (2 * side + kind) * hidden : (2 * side + kind + 1) * hidden], NT,
                preferred_element_type=F32,
            )
            for side in range(2)
        )
        proj_s[2 * kind * hidden : 2 * (kind + 1) * hidden] = (rows * (1.0 - 0.5 * (1 - kind))).astype(BF16)
    proj_s[wide:] = (weight_ref[...].astype(F32).T * 0.5).astype(BF16)


def emit_factors(rows_z, first, pair_mask_s, gain_s, proj_s, ab_ref, z_ref, gate_ref, groups):
    nodes = pair_mask_s.shape[1]
    half = ab_ref.shape[1] // z_ref.shape[0] * groups
    for r in range(0, len(rows_z), 2):
        normed = [norm_channels(z.astype(F32), gain_s[...]).astype(BF16) for z in rows_z[r : r + 2]]
        half_rows = proj_s.shape[0] - 2 * half
        masked = [n * pair_mask_s[first + r + i : first + r + i + 1, :].astype(BF16) for i, n in enumerate(normed)]
        plain = jnp.concatenate(normed, axis=1)
        gates = dot(proj_s[:half], plain)
        values = dot(proj_s[half : 2 * half], jnp.concatenate(masked, axis=1))
        outs = dot(proj_s[2 * half :], plain)
        done = []
        for i in range(2):
            row = first + r + i
            part = slice(i * nodes, (i + 1) * nodes)
            z_ref[row] = rows_z[r + i]
            gate_ref[row] = jnp.tanh(outs[:, part]) * 0.5 + 0.5
            ab = (jnp.tanh(gates[:, part]) + 1.0) * values[:, part]
            done.append(ab.reshape(groups, half // groups, nodes))
        both = jnp.concatenate(done, axis=1).astype(BF16)
        height = both.shape[1]
        at = (first + r) // 2 * height
        ab_ref[:, at : at + height, :] = both


def start_all(pairs, sems):
    copies = [pltpu.make_async_copy(source, target, sems.at[i]) for i, (source, target) in enumerate(pairs)]
    for copy in copies:
        copy.start()
    return copies


def chunk(ref, at):
    return ref.at[pl.ds(at * STEP, STEP)]


def row_masks(mask_ref, rows):
    nodes = mask_ref.shape[0]
    lanes = mask_ref[...].reshape(1, nodes).astype(F32)
    row, col = iotas(16, nodes)
    own = jnp.where(col == lax.axis_index("row") * rows + row, lanes, 0.0)
    return jnp.sum(own, axis=1, keepdims=True) * (lanes * 0.5)


def embedded_rows(step, pair_ref, edge_ref, table):
    chans, kinds = table.shape
    nodes = edge_ref.shape[1]
    ident = eye(chans)
    rows_z = []
    for r in range(0, STEP, 2):
        edges = jnp.concatenate([edge_ref[pl.ds(step * STEP + r + i, 1), :] for i in range(2)], axis=1)
        onehot = (lax.broadcasted_iota(jnp.int32, (kinds, 2 * nodes), 0) == edges).astype(BF16)
        added = dot(table, onehot)
        pair = lax.dot_general(
            ident, pair_ref[r : r + 2].reshape(2 * nodes, chans), NT, preferred_element_type=F32
        )
        z = (pair + added).astype(BF16)
        rows_z += [z[:, :nodes], z[:, nodes:]]
    return rows_z


def first_kernel(
    pair_hbm, edge_hbm, mask_hbm, table_hbm, gain_hbm, proj_hbm, weight_hbm, out_gain_hbm, out_weight_hbm,
    ab_ref, z_ref, gate_ref, gain_s, proj_s, pair_mask_s, out_gain_s, out_weight_s,
    pair_ref, edge_ref, mask_ref, table_ref, gain_ref, proj_ref, weight_ref, out_gain_ref, out_weight_ref, sems,
):
    rows, groups = pair_ref.shape[0], ab_ref.shape[0]
    small = [
        (gain_hbm, gain_ref), (proj_hbm, proj_ref), (weight_hbm, weight_ref), (table_hbm, table_ref),
        (mask_hbm, mask_ref), (edge_hbm, edge_ref), (out_gain_hbm, out_gain_ref), (out_weight_hbm, out_weight_ref),
    ]
    large = [(chunk(pair_hbm, at), chunk(pair_ref, at)) for at in range(rows // STEP)]
    copies = start_all(small + large, sems)
    for copy in copies[: len(small)]:
        copy.wait()
    for layer in range(2):
        prepare_in(
            gain_ref, proj_ref.at[layer], weight_ref.at[layer], gain_s.at[layer], proj_s.at[layer], layer, groups
        )
        prepare_out(out_gain_ref, out_weight_ref.at[layer], out_gain_s.at[layer], out_weight_s.at[layer], layer)
    table = table_ref[...].astype(F32).T.astype(BF16)
    pair_mask_s[...] = row_masks(mask_ref, rows)
    for at in range(rows // STEP):
        copies[len(small) + at].wait()
        rows_z = embedded_rows(at, chunk(pair_ref, at), edge_ref, table)
        emit_factors(rows_z, at * STEP, pair_mask_s, gain_s.at[0], proj_s.at[0], ab_ref, z_ref, gate_ref, groups)


def prepare_out(gain_ref, weight_ref, gain_s, weight_s, layer):
    chans = gain_ref.shape[1]
    gain = jnp.broadcast_to(gain_ref[layer : layer + 1, :], (chans, chans)).T
    gain_s[...] = jnp.concatenate([gain] * (gain_s.shape[1] // chans), axis=1)
    weight_s[...] = weight_ref[...].astype(F32).T.astype(BF16)


def products_of(tri_ref, at):
    groups, _, nodes = tri_ref.shape
    height = STEP * 4
    per = 128 // groups
    eight = 128 // height
    row, col = iotas(128, 128)
    wide = eight * per
    pick = (col == ((row % wide) // per) * height + (row // wide) * per + row % per).astype(BF16)
    blocks = [
        tri_ref[q * eight : (q + 1) * eight, at * height : (at + 1) * height, :].reshape(128, nodes)
        for q in range(groups // eight)
    ]
    parts = []
    for q in range(0, groups // eight, 2):
        moved = dot(pick, jnp.concatenate(blocks[q : q + 2], axis=1))
        parts += [moved[:, :nodes], moved[:, nodes:]]
    return [
        jnp.concatenate([p[r * wide : (r + 1) * wide] for p in parts], axis=0) for r in range(STEP)
    ]


def updated_rows(products, z_ref, gate_ref, gain_s, weight_s):
    rows_z = []
    nodes = z_ref.shape[2]
    for r in range(0, STEP, 2):
        tri_norm = [norm_channels(tri, gain_s[...]).astype(BF16) for tri in products[r : r + 2]]
        update = dot(weight_s[...], jnp.concatenate(tri_norm, axis=1))
        for i in range(2):
            rows_z.append(
                (z_ref[r + i].astype(F32) + gate_ref[r + i] * update[:, i * nodes : (i + 1) * nodes]).astype(BF16)
            )
    return rows_z


def middle_kernel(
    tri_ref, zin_ref, gin_ref, gain_s, proj_s, pair_mask_s, out_gain_s, out_weight_s, ab_ref, z_ref, gate_ref
):
    rows, groups = zin_ref.shape[0], ab_ref.shape[0]
    for at in range(rows // STEP):
        rows_z = updated_rows(
            products_of(tri_ref, at), chunk(zin_ref, at), chunk(gin_ref, at), out_gain_s.at[0], out_weight_s.at[0]
        )
        emit_factors(rows_z, at * STEP, pair_mask_s, gain_s.at[1], proj_s.at[1], ab_ref, z_ref, gate_ref, groups)


def last_kernel(tri_ref, z_ref, gate_ref, out_gain_s, out_weight_s, result_hbm, result_ref, out_sems):
    rows = z_ref.shape[0]
    ident = eye(tri_ref.shape[2])
    sent = []
    for at in range(rows // STEP):
        rows_z = updated_rows(
            products_of(tri_ref, at), chunk(z_ref, at), chunk(gate_ref, at), out_gain_s.at[1], out_weight_s.at[1]
        )
        for r in range(0, STEP, 2):
            turned = lax.dot_general(
                ident, jnp.concatenate(rows_z[r : r + 2], axis=0), NT, preferred_element_type=F32
            ).astype(BF16)
            chans = turned.shape[1] // 2
            result_ref[at * STEP + r] = turned[:, :chans]
            result_ref[at * STEP + r + 1] = turned[:, chans:]
            pair = pl.ds(at * STEP + r, 2)
            copy = pltpu.make_async_copy(result_ref.at[pair], result_hbm.at[pair], out_sems.at[len(sent)])
            copy.start()
            sent.append(copy)
    for copy in sent:
        copy.wait()


def triangle_kernel(ab_ref, tri_ref, sides_s, tri_s, *, layer):
    kinds, nodes, _ = sides_s.shape
    per = kinds // 2
    high = 128 // kinds
    pick = swap_matrix(128, kinds, high)
    for at in range(nodes // high):
        moved = dot(pick, ab_ref[at * 128 : (at + 1) * 128, :]).astype(BF16)
        for kind in range(kinds):
            sides_s[kind, at * high : (at + 1) * high, :] = moved[kind * high : (kind + 1) * high]
    for c in range(per):
        left, right = sides_s[c], sides_s[per + c]
        tri_s[c] = lax.dot_general(
            left, right, NT if layer == 0 else TN, preferred_element_type=F32
        ).astype(BF16)
    low = 128 // per
    back = swap_matrix(128, low, per)
    for at in range(nodes // low):
        stacked = tri_s[:, at * low : (at + 1) * low, :].reshape(128, nodes)
        tri_ref[at * 128 : (at + 1) * 128, :] = dot(back, stacked).astype(BF16)


LIMIT = 32 * 1024 * 1024


def in_hbm(array):
    return pltpu.with_memory_space_constraint(array, pltpu.HBM)


def in_vmem(array):
    return pltpu.with_memory_space_constraint(array, pltpu.VMEM)


def whole(array):
    zeros = (0,) * array.ndim
    return pl.BlockSpec(array.shape, lambda i: zeros)


def body(
    pair, edge_type, node_mask, type_table, in_gain, proj_weight, gate_weight, out_gain, out_weight
):
    rows, nodes, chans = pair.shape
    hidden = out_weight.shape[1]
    groups = lax.axis_size("row")
    per = hidden // groups
    steps = rows // STEP
    node_mask = in_hbm(node_mask)
    params = pltpu.CompilerParams(vmem_limit_bytes=LIMIT)

    def by_row(*shape):
        return pl.BlockSpec((STEP, *shape), lambda i: (i, 0, 0))

    anywhere = pl.BlockSpec(memory_space=pl.ANY)
    vmem = pl.BlockSpec(memory_space=pltpu.VMEM)
    factors = pltpu.VMEM((groups, rows * 2 * per, nodes), BF16)
    emitted = [factors, pltpu.VMEM((rows, chans, nodes), BF16), pltpu.VMEM((rows, chans, nodes), F32)]
    pair, edge_type, type_table, in_gain, proj_weight, gate_weight, out_gain, out_weight = (
        in_hbm(x)
        for x in (pair, edge_type, type_table, in_gain, proj_weight, gate_weight, out_gain, out_weight)
    )
    prepared = [
        pltpu.VMEM((2, chans, nodes), F32), pltpu.VMEM((2, 4 * hidden + chans, chans), BF16),
        pltpu.VMEM((16, nodes), F32), pltpu.VMEM((2, hidden, nodes), F32), pltpu.VMEM((2, chans, hidden), BF16),
    ]

    def sems(count):
        return pltpu.SemaphoreType.DMA((count,))

    def triangle(ab, layer):
        sent = lax.all_to_all(ab, "row", split_axis=0, concat_axis=0, tiled=True)
        tri = pl.pallas_call(
            lambda *refs: triangle_kernel(*refs, layer=layer),
            out_shape=pltpu.VMEM((nodes * per, nodes), BF16),
            in_specs=[vmem],
            out_specs=vmem,
            scratch_shapes=[pltpu.VMEM((2 * per, nodes, nodes), BF16), pltpu.VMEM((per, nodes, nodes), BF16)],
            compiler_params=params,
        )(in_vmem(sent.reshape(nodes * 2 * per, nodes)))
        return lax.all_to_all(
            tri.reshape(groups, rows * per, nodes), "row", split_axis=0, concat_axis=0, tiled=True
        )

    arguments = (
        pair, edge_type, node_mask, type_table, in_gain, proj_weight, gate_weight, out_gain, out_weight
    )
    ab, z, gate, *weights = pl.pallas_call(
        first_kernel,
        out_shape=emitted + prepared,
        in_specs=[anywhere] * 9,
        out_specs=[vmem] * 8,
        scratch_shapes=[*(pltpu.VMEM(x.shape, x.dtype) for x in arguments), sems(8 + steps)],
        compiler_params=params,
    )(*arguments)
    weights = [in_vmem(x) for x in weights]
    tri = triangle(ab, 0)
    ab, z, gate = pl.pallas_call(
        middle_kernel,
        out_shape=emitted,
        in_specs=[vmem] * 8,
        out_specs=[vmem] * 3,
        compiler_params=params,
    )(in_vmem(tri), in_vmem(z), in_vmem(gate), *weights)
    tri = triangle(ab, 1)
    return pl.pallas_call(
        last_kernel,
        out_shape=pltpu.HBM((rows, nodes, chans), BF16),
        in_specs=[vmem] * 5,
        out_specs=anywhere,
        scratch_shapes=[pltpu.VMEM((rows, nodes, chans), BF16), sems(rows // 2)],
        compiler_params=params,
    )(in_vmem(tri), in_vmem(z), in_vmem(gate), *weights[3:])


def solution(mesh):
    in_specs = (
        P(("graph", "row"), None, None),
        P(("graph", "row"), None),
        P("graph"),
        P(),
        P(),
        P(),
        P(),
        P(),
        P(),
    )
    out_specs = P(("graph", "row"), None, None)
    return jax.shard_map(body, mesh=mesh, in_specs=in_specs, out_specs=out_specs, check_vma=False)
```
